32 devices in a mesh: row: 4 (over x, core), col: 8 (over z, y).
Axes of the slice: x: 2, y: 2, z: 4, core: 2. Of those that a mesh axis runs over, the one named last changes fastest.
Arguments:
- tokens: bfloat16 [512, 12288], P('col', 'row'), may hold values from -6 to 6
- up_mant: bfloat16 [12288, 24576], P('row', 'col'), may hold values from -0.0546875 to 0.0546875
- up_exp: int32 [24576], P('col'), may hold values from -1 to 1
- down_mant: bfloat16 [24576, 12288], P('col', 'row'), may hold values from -0.0390625 to 0.0390625
- down_exp: int32 [12288], P('row'), may hold values from -1 to 1
- cotangent: bfloat16 [512, 12288], P('col', 'row'), may hold values from -6 to 6
Outputs:
- output: bfloat16 [512, 12288], P('col', 'row')
- grad_tokens: bfloat16 [512, 12288], P('col', 'row')
- grad_up: bfloat16 [12288, 24576], P('row', 'col')
- grad_down: bfloat16 [24576, 12288], P('col', 'row')
The draws below stay inside these ranges and needn't reach their ends.
All inputs are finite; a program needn't handle non-finite values.
Results may differ from the reference program's by a relative error of at most 0.018.
Values may be sent and summed in bfloat16 or wider, within the bound.
A program may use at most 192 MiB of HBM per device.

```python
import jax
import jax.numpy as jnp
from jax import lax

D = 12288
FF = 24576
TOKENS = 512
N_ROW = 4
N_COL = 8


def place_ends(values, stream_key, least, top_value):
    place = [jax.random.randint(jax.random.fold_in(stream_key, axis), (), 0, length) for axis, length in enumerate(values.shape)]
    widest = values.shape.index(max(values.shape))
    neighbour = place[:widest] + [(place[widest] + 1) % values.shape[widest]] + place[widest + 1:]
    return values.at[tuple(place)].set(least).at[tuple(neighbour)].set(top_value)


def steps_of(rng, shape, pieces, low, high):
    gain = 1.0
    for axis_at, blocks in pieces:
        draws = jax.random.uniform(jax.random.fold_in(jax.random.fold_in(rng, 6), axis_at), (blocks,), jnp.float32, low / len(pieces), high / len(pieces))
        gain = gain * jnp.repeat(jnp.exp(draws), shape[axis_at] // blocks).reshape((-1,) + (1,) * (len(shape) - 1 - axis_at))
    return gain


def gaussian(own_key, shape, scale, bound, pieces=(), kind=jnp.bfloat16):
    values = scale * jax.random.normal(own_key, shape, jnp.float32)
    if pieces:
        values = values * steps_of(own_key, shape, pieces, -0.22, 0.18)
    return jnp.clip(values, -bound, bound).astype(kind)


def setup_inputs(seed: int = 0) -> dict:
    key_of = jax.random.split(jax.random.key(seed), 7)
    tokens = gaussian(key_of[0], (TOKENS, D), 1.0, 6.0, ((0, 8), (1, 4)))
    up_mant = gaussian(key_of[1], (D, FF), D ** -0.5, 0.0546875, ((0, 4), (1, 8)))
    up_exp = place_ends(jax.random.randint(key_of[2], (FF,), -1, 2), jax.random.fold_in(key_of[2], 1), -1, 1).astype(jnp.int32)
    down_mant = gaussian(key_of[3], (FF, D), FF ** -0.5, 0.0390625, ((0, 8), (1, 4)))
    down_exp = place_ends(jax.random.randint(key_of[4], (D,), -1, 2), jax.random.fold_in(key_of[4], 1), -1, 1).astype(jnp.int32)
    cotangent = gaussian(key_of[5], (TOKENS, D), 1.0, 6.0, ((0, 8), (1, 4)))
    return dict(tokens=tokens, up_mant=up_mant, up_exp=up_exp, down_mant=down_mant, down_exp=down_exp, cotangent=cotangent)


def blocked_product(left, right, nblocks):
    rows = left.shape[0]
    inner = left.shape[1]
    width = inner // nblocks
    left_blocks = left.reshape(rows, nblocks, width).transpose(1, 0, 2)
    right_blocks = right.reshape(nblocks, width, right.shape[1])

    def add_block(total, pair):
        term = jnp.dot(pair[0], pair[1], preferred_element_type=jnp.float32).astype(jnp.bfloat16)
        term = lax.optimization_barrier(term)
        return (total + term.astype(jnp.float32), None)
    start = jnp.zeros((rows, right.shape[1]), jnp.float32)
    total, _ = lax.scan(add_block, start, (left_blocks, right_blocks))
    return total

def gelu_grad(pre_act, upstream):
    return jax.vjp(jax.nn.gelu, pre_act)[1](upstream)[0]

def reference(tokens, up_mant, up_exp, down_mant, down_exp, cotangent):
    up_scale = jnp.exp2(up_exp.astype(jnp.float32))
    down_scale = jnp.exp2(down_exp.astype(jnp.float32))
    pre_act = blocked_product(tokens, up_mant, N_ROW) * up_scale[None, :]
    hidden = jax.nn.gelu(pre_act).astype(jnp.bfloat16)
    output = (blocked_product(hidden, down_mant, N_COL) * down_scale[None, :]).astype(jnp.bfloat16)
    grad_out = (cotangent.astype(jnp.float32) * down_scale[None, :]).astype(jnp.bfloat16)
    grad_down = jnp.dot(hidden.T, grad_out, preferred_element_type=jnp.float32).astype(jnp.bfloat16)
    grad_hidden = blocked_product(grad_out, down_mant.T, N_ROW)
    grad_mid = (gelu_grad(pre_act, grad_hidden) * up_scale[None, :]).astype(jnp.bfloat16)
    grad_up = jnp.dot(tokens.T, grad_mid, preferred_element_type=jnp.float32).astype(jnp.bfloat16)
    grad_tokens = blocked_product(grad_mid, up_mant.T, N_COL).astype(jnp.bfloat16)
    return (output, grad_tokens, grad_up, grad_down)
```

```python
import functools
import math

import jax
import jax.numpy as jnp
from jax import lax
from jax.experimental import pallas as pl
from jax.experimental.pallas import tpu as pltpu
from jax.sharding import PartitionSpec as P

MESH = pl.DeviceIdType.MESH
F32 = jnp.float32
BF16 = jnp.bfloat16
ROWS = 16
ROOT = math.sqrt(2.0 / math.pi)
CUBIC = 0.044715


def remote(src, dst, send, recv, where):
    return pltpu.make_async_remote_copy(
        src_ref=src, dst_ref=dst, send_sem=send, recv_sem=recv, device_id=where, device_id_type=MESH
    )


def band(index, size):
    return pl.ds(pl.multiple_of(index * size, size), size)


def tiles(rows, body):
    def step(i, carry):
        body(pl.ds(pl.multiple_of(i * ROWS, ROWS), ROWS), i)
        return carry

    lax.fori_loop(0, rows // ROWS, step, 0)


class Ring:
    def __init__(self, n):
        self.n = n
        col = lax.axis_index("col")
        self.col = col
        half = col // 2
        odd = lax.rem(col, 2)
        self.pos = half + odd * (n - 1 - 2 * half)
        self.right = {"col": self.at(1)}
        self.left = {"col": self.at(-1)}

    def at(self, shift):
        q = lax.rem(self.pos + shift + 2 * self.n, self.n)
        return jnp.where(q < self.n // 2, 2 * q, 2 * (self.n - 1 - q) + 1)


class Rows:
    def __init__(self, count):
        self.groups = count // 2
        me = lax.axis_index("row")
        self.me = me
        self.core = lax.rem(me, 2)
        self.group = me // 2
        self.sibling = {"row": me + 1 - 2 * self.core}

    def of(self, shift, core):
        return lax.rem(self.group + shift + 2 * self.groups, self.groups) * 2 + core


def greet(ring, rows):
    partners = []
    if ring is not None:
        partners += [ring.left, ring.right]
    if rows is not None:
        partners += [rows.sibling]
        partners += [{"row": rows.of(d, rows.core)} for d in range(1, rows.groups)]
    barrier = pltpu.get_barrier_semaphore()
    for partner in partners:
        pl.semaphore_signal(barrier, inc=1, device_id=partner, device_id_type=MESH)
    pl.semaphore_wait(barrier, len(partners))


class RingGather:
    def __init__(self, ring, full, send, recv):
        self.ring, self.full, self.send, self.recv = ring, full, send, recv
        self.m = full.shape[0] // ring.n
        self.w = full.shape[1] // 2
        self.last = ring.n // 2 - 1
        self.sent = []
        self.now = None

    def start(self, step):
        ring = self.ring
        self.now = {}
        for way in range(2):
            origin = ring.at(-step if way == 0 else step)
            for h in range(2):
                if step == self.last and h != way:
                    continue
                part = self.full.at[band(origin, self.m), pl.ds(h * self.w, self.w)]
                copy = remote(
                    part, part, self.send.at[way, h, step], self.recv.at[way, h, step],
                    ring.right if way == 0 else ring.left,
                )
                copy.start()
                self.now[way, h] = copy
                self.sent.append(copy)

    def step(self, step):
        ring = self.ring
        before = self.now
        self.now = {}
        for h in range(2):
            for way in range(2):
                before[way, h].wait_recv()
                if step == self.last and h != way:
                    continue
                origin = ring.at(-step if way == 0 else step)
                part = self.full.at[band(origin, self.m), pl.ds(h * self.w, self.w)]
                copy = remote(
                    part, part, self.send.at[way, h, step], self.recv.at[way, h, step],
                    ring.right if way == 0 else ring.left,
                )
                copy.start()
                self.now[way, h] = copy
                self.sent.append(copy)

    def finish(self):
        for copy in self.now.values():
            copy.wait_recv()
        for copy in self.sent:
            copy.wait_send()


def ring_gather_sems(n):
    return [pltpu.SemaphoreType.DMA((2, 2, n // 2))] * 2


def lanes(width):
    return 2 if (width // 4) % 128 == 0 else 1


class RingScatter:
    def __init__(self, ring, part, slots, send, recv):
        self.ring, self.part, self.slots, self.send, self.recv = ring, part, slots, send, recv
        self.m = part.shape[0] // ring.n
        self.k = lanes(part.shape[1])
        self.w = part.shape[1] // (2 * self.k)
        self.sent = []
        self.now = {}

    def columns(self, way, j):
        return pl.ds((way * self.k + j) * self.w, self.w)

    def start(self, step):
        ring = self.ring
        before, self.now = self.now, {}
        for j in range(self.k):
            for way in range(2):
                dest = ring.at(-1 - step if way == 0 else 1 + step)
                own = self.part.at[band(dest, self.m), self.columns(way, j)]
                src = own
                if step > 0:
                    before[way, j].wait_recv()
                    src = self.slots.at[way, step - 1, j]

                    def add(at, i, src=src, own=own):
                        src[at, :] = (src[at, :].astype(F32) + own[at, :].astype(F32)).astype(BF16)

                    tiles(self.m, add)
                copy = remote(
                    src, self.slots.at[way, step, j], self.send.at[way, j, step],
                    self.recv.at[way, j, step], ring.right if way == 0 else ring.left,
                )
                copy.start()
                self.now[way, j] = copy
                self.sent.append(copy)

    def finish(self, scale, out):
        ring = self.ring
        for j in range(self.k):
            for way in range(2):
                self.now[way, j].wait_recv()
                own = self.part.at[band(ring.col, self.m), self.columns(way, j)]
                got = self.slots.at[way, ring.n - 2, j]
                columns = self.columns(way, j)

                def add(at, i, own=own, got=got, columns=columns):
                    total = got[at, :].astype(F32) + own[at, :].astype(F32)
                    if scale is not None:
                        total = total * scale[0:1, columns]
                    out[at, columns] = total.astype(BF16)

                tiles(self.m, add)
        for copy in self.sent:
            copy.wait_send()


def ring_scatter_scratch(n, tokens, width):
    k = lanes(width)
    return [
        pltpu.VMEM((2, n - 1, k, tokens // n, width // (2 * k)), BF16),
        pltpu.SemaphoreType.DMA((2, k, n - 1)),
        pltpu.SemaphoreType.DMA((2, k, n - 1)),
    ]


class RowScatter:
    def __init__(self, rows, part, sib, out, land, send, recv):
        self.rows, self.part, self.sib, self.out, self.land = rows, part, sib, out, land
        self.send, self.recv = send, recv
        self.m = part.shape[0] // (2 * rows.groups)

    def pairs(self):
        rows = self.rows
        g = rows.groups
        self.first = []
        for d in [*range(1, g), 0]:
            chunk = rows.of(d, 1 - rows.core)
            copy = remote(
                self.part.at[band(chunk, self.m), :], self.sib.at[d], self.send.at[0, d],
                self.recv.at[0, d], rows.sibling,
            )
            copy.start()
            self.first.append((d, copy))

    def chips(self):
        rows = self.rows
        self.second = []
        for d, copy in self.first:
            copy.wait_recv()
            if d == 0:
                continue
            own = self.part.at[band(rows.of(d, rows.core), self.m), :]

            def add(at, i, d=d, own=own):
                self.out[d - 1, at, :] = (
                    own[at, :].astype(F32) + self.sib[d, at, :].astype(F32)
                ).astype(BF16)

            tiles(self.m, add)
            far = remote(
                self.out.at[d - 1], self.land.at[d - 1], self.send.at[1, d], self.recv.at[1, d],
                {"row": rows.of(d, rows.core)},
            )
            far.start()
            self.second.append(far)

    def arrived(self):
        for copy in self.second:
            copy.wait_recv()

    def total(self, at, i):
        m = self.m
        own = pl.ds(pl.multiple_of(self.rows.me * m + i * ROWS, ROWS), ROWS)
        value = self.part[own, :].astype(F32) + self.sib[0, at, :].astype(F32)
        for d in range(1, self.rows.groups):
            value += self.land[d - 1, at, :].astype(F32)
        return value

    def finish(self):
        for _, copy in self.first:
            copy.wait_send()
        for copy in self.second:
            copy.wait_send()


def row_scratch(count, tokens, width):
    g = count // 2
    m = tokens // count
    return [
        pltpu.VMEM((g, m, width), BF16),
        pltpu.VMEM((max(g - 1, 1), m, width), BF16),
        pltpu.VMEM((max(g - 1, 1), m, width), BF16),
    ] + [pltpu.SemaphoreType.DMA((2, g))] * 4


class RowGather:
    def __init__(self, rows, full, send, recv):
        self.rows, self.full, self.send, self.recv = rows, full, send, recv
        self.m = full.shape[0] // (2 * rows.groups)

    def to_sibling(self, d):
        part = self.full.at[band(self.rows.of(-d, self.rows.core), self.m), :]
        copy = remote(part, part, self.send.at[0, d], self.recv.at[0, d], self.rows.sibling)
        copy.start()
        return copy

    def start(self):
        rows = self.rows
        part = self.full.at[band(rows.me, self.m), :]
        self.far = []
        for d in range(1, rows.groups):
            copy = remote(
                part, part, self.send.at[1, d], self.recv.at[1, d], {"row": rows.of(d, rows.core)}
            )
            copy.start()
            self.far.append(copy)
        self.near = [self.to_sibling(0)]

    def finish(self):
        for d, copy in enumerate(self.far, 1):
            copy.wait_recv()
            self.near.append(self.to_sibling(d))
        for copy in self.near:
            copy.wait_recv()
        for copy in self.near + self.far:
            copy.wait_send()


def interleave(gather_step, count, row_scatter, middle, row_gather):
    row_scatter.pairs()
    row_scatter.chips()
    half = (2 * count + 2) // 3
    for s in range(1, 1 + half):
        gather_step(s)
    row_scatter.arrived()
    middle()
    row_gather.start()
    for s in range(1 + half, count + 1):
        gather_step(s)


def tokens_kernel(n, share, full, send, recv):
    ring = Ring(n)
    m = share.shape[0]
    full[band(ring.col, m), :] = share[...]
    greet(ring, None)
    gather = RingGather(ring, full, send, recv)
    gather.start(0)
    for s in range(1, n // 2):
        gather.step(s)
    gather.finish()


def forward_kernel(
    n, count, part, share, up_scale, down_scale, hidden, grad_out, pre,
    send, recv, sib, out, land, rs_send, rs_recv, ag_send, ag_recv,
):
    ring, rows = Ring(n), Rows(count)
    m = share.shape[0]
    grad_out[band(ring.col, m), :] = (share[...].astype(F32) * down_scale[0:1, :]).astype(BF16)
    greet(ring, rows)
    scatter = RowScatter(rows, part, sib, out, land, rs_send, rs_recv)
    row_gather = RowGather(rows, hidden, ag_send, ag_recv)
    gather = RingGather(ring, grad_out, send, recv)
    gather.start(0)
    mr = scatter.m

    def middle():
        def body(at, i):
            x = scatter.total(at, i) * up_scale[0:1, :]
            pre[at, :] = x
            h = 0.5 * x * (1.0 + jnp.tanh(ROOT * (x + CUBIC * (x * x * x))))
            mine = pl.ds(pl.multiple_of(rows.me * mr + i * ROWS, ROWS), ROWS)
            hidden[mine, :] = h.astype(BF16)

        tiles(mr, body)

    interleave(gather.step, n // 2 - 1, scatter, middle, row_gather)
    row_gather.finish()
    gather.finish()
    scatter.finish()


def backward_kernel(
    n, count, part, out_part, pre, up_scale, down_scale, mid, output,
    slots, send, recv, sib, out, land, rs_send, rs_recv, ag_send, ag_recv,
):
    ring, rows = Ring(n), Rows(count)
    greet(ring, rows)
    scatter = RowScatter(rows, part, sib, out, land, rs_send, rs_recv)
    row_gather = RowGather(rows, mid, ag_send, ag_recv)
    sums = RingScatter(ring, out_part, slots, send, recv)
    sums.start(0)
    mr = scatter.m

    def middle():
        def body(at, i):
            up = scatter.total(at, i)
            x = pre[at, :]
            t = jnp.tanh(ROOT * (x + CUBIC * (x * x * x)))
            slope = 0.5 * (1.0 + t) + 0.5 * x * (1.0 - t * t) * (ROOT * (1.0 + 3.0 * CUBIC * (x * x)))
            mine = pl.ds(pl.multiple_of(rows.me * mr + i * ROWS, ROWS), ROWS)
            mid[mine, :] = (slope * up * up_scale[0:1, :]).astype(BF16)

        tiles(mr, body)

    interleave(sums.start, n - 2, scatter, middle, row_gather)
    row_gather.finish()
    sums.finish(down_scale, output)
    scatter.finish()


def sum_kernel(n, part, result, slots, send, recv):
    ring = Ring(n)
    greet(ring, None)
    sums = RingScatter(ring, part, slots, send, recv)
    for s in range(n - 1):
        sums.start(s)
    sums.finish(None, result)


def call(body, outs, scratch, number, *operands):
    spec = pl.BlockSpec(memory_space=pltpu.VMEM)
    return pl.pallas_call(
        body,
        out_shape=outs,
        in_specs=[spec] * len(operands),
        out_specs=jax.tree.map(lambda _: spec, outs),
        scratch_shapes=scratch,
        compiler_params=pltpu.CompilerParams(
            collective_id=number, has_side_effects=True, vmem_limit_bytes=48 * 1024 * 1024
        ),
    )(*operands)


def outer_kernel(step, left, right, out):
    def body(j, carry):
        at = pl.ds(pl.multiple_of(j * step, step), step)
        out[:, at] = lax.dot_general(
            left[...], right[:, at], (((0,), (0,)), ((), ())), preferred_element_type=F32
        ).astype(BF16)
        return carry

    lax.fori_loop(0, right.shape[1] // step, body, 0)


def outer(left, right):
    tokens, a = left.shape
    b = right.shape[1]
    ta, tb = math.gcd(a, 512), math.gcd(b, 1024)
    return pl.pallas_call(
        functools.partial(outer_kernel, tb),
        out_shape=jax.ShapeDtypeStruct((a, b), BF16),
        grid=(a // ta,),
        in_specs=[
            pl.BlockSpec((tokens, ta), lambda i: (0, i)),
            pl.BlockSpec((tokens, b), lambda i: (0, 0)),
        ],
        out_specs=pl.BlockSpec((ta, b), lambda i: (i, 0)),
        compiler_params=pltpu.CompilerParams(vmem_limit_bytes=40 * 1024 * 1024),
        cost_estimate=pl.CostEstimate(
            flops=2 * a * b * tokens, bytes_accessed=2 * (a * b + tokens * (a + b)), transcendentals=0
        ),
    )(left, right)


def shards(n, count, tokens, up_mant, up_exp, down_mant, down_exp, cotangent):
    struct = jax.ShapeDtypeStruct
    m, width = tokens.shape
    units = up_mant.shape[1]
    total = m * n
    up_scale = jnp.exp2(up_exp.astype(F32))[None, :]
    down_scale = jnp.exp2(down_exp.astype(F32))[None, :]
    x_full = call(
        functools.partial(tokens_kernel, n), struct((total, width), BF16), ring_gather_sems(n), 0, tokens
    )
    up_term = jnp.dot(x_full, up_mant, preferred_element_type=F32).astype(BF16)
    hidden, grad_out, pre = call(
        functools.partial(forward_kernel, n, count),
        (struct((total, units), BF16), struct((total, width), BF16), struct((total // count, units), F32)),
        ring_gather_sems(n) + row_scratch(count, total, units),
        1, up_term, cotangent, up_scale, down_scale,
    )
    out_term = jnp.dot(hidden, down_mant, preferred_element_type=F32).astype(BF16)
    back_term = lax.dot_general(
        grad_out, down_mant, (((1,), (1,)), ((), ())), preferred_element_type=F32
    ).astype(BF16)
    mid, output = call(
        functools.partial(backward_kernel, n, count),
        (struct((total, units), BF16), struct((m, width), BF16)),
        ring_scatter_scratch(n, total, width) + row_scratch(count, total, units),
        2, back_term, out_term, pre, up_scale, down_scale,
    )
    tokens_term = lax.dot_general(
        mid, up_mant, (((1,), (1,)), ((), ())), preferred_element_type=F32
    ).astype(BF16)
    grad_tokens = call(
        functools.partial(sum_kernel, n), struct((m, width), BF16),
        ring_scatter_scratch(n, total, width), 3, tokens_term,
    )
    return (output, grad_tokens, outer(x_full, mid), outer(hidden, grad_out))


def solution(mesh):
    placed = (P("col", "row"), P("row", "col"), P("col"), P("col", "row"), P("row"), P("col", "row"))
    return jax.shard_map(
        functools.partial(shards, mesh.shape["col"], mesh.shape["row"]),
        mesh=mesh,
        in_specs=placed,
        out_specs=(P("col", "row"), P("col", "row"), P("row", "col"), P("col", "row")),
        check_vma=False,
    )
```

```python
import functools
import math

import jax
import jax.numpy as jnp
from jax import lax
from jax.experimental import pallas as pl
from jax.experimental.pallas import tpu as pltpu
from jax.sharding import PartitionSpec as P

MESH = pl.DeviceIdType.MESH
F32 = jnp.float32
BF16 = jnp.bfloat16
ROWS = 16
ROOT = math.sqrt(2.0 / math.pi)
CUBIC = 0.044715


def remote(src, dst, send, recv, where):
    return pltpu.make_async_remote_copy(
        src_ref=src, dst_ref=dst, send_sem=send, recv_sem=recv, device_id=where, device_id_type=MESH
    )


def band(index, size):
    return pl.ds(pl.multiple_of(index * size, size), size)


def tiles(rows, body):
    def step(i, carry):
        body(pl.ds(pl.multiple_of(i * ROWS, ROWS), ROWS), i)
        return carry

    lax.fori_loop(0, rows // ROWS, step, 0)


class Ring:
    def __init__(self, n):
        self.n = n
        col = lax.axis_index("col")
        self.col = col
        half = col // 2
        odd = lax.rem(col, 2)
        self.pos = half + odd * (n - 1 - 2 * half)
        self.right = {"col": self.at(1)}
        self.left = {"col": self.at(-1)}

    def at(self, shift):
        q = lax.rem(self.pos + shift + 2 * self.n, self.n)
        return jnp.where(q < self.n // 2, 2 * q, 2 * (self.n - 1 - q) + 1)


class Rows:
    def __init__(self, count):
        self.groups = count // 2
        me = lax.axis_index("row")
        self.me = me
        self.core = lax.rem(me, 2)
        self.group = me // 2
        self.sibling = {"row": me + 1 - 2 * self.core}

    def of(self, shift, core):
        return lax.rem(self.group + shift + 2 * self.groups, self.groups) * 2 + core


def greet(ring, rows):
    partners = []
    if ring is not None:
        partners += [ring.left, ring.right]
    if rows is not None:
        partners += [rows.sibling]
        partners += [{"row": rows.of(d, rows.core)} for d in range(1, rows.groups)]
    barrier = pltpu.get_barrier_semaphore()
    for partner in partners:
        pl.semaphore_signal(barrier, inc=1, device_id=partner, device_id_type=MESH)
    pl.semaphore_wait(barrier, len(partners))


class RingGather:
    def __init__(self, ring, full, send, recv):
        self.ring, self.full, self.send, self.recv = ring, full, send, recv
        self.m = full.shape[0] // ring.n
        self.w = full.shape[1] // 2
        self.last = ring.n // 2 - 1
        self.sent = []
        self.now = None

    def start(self, step):
        ring = self.ring
        self.now = {}
        for way in range(2):
            origin = ring.at(-step if way == 0 else step)
            for h in range(2):
                if step == self.last and h != way:
                    continue
                part = self.full.at[band(origin, self.m), pl.ds(h * self.w, self.w)]
                copy = remote(
                    part, part, self.send.at[way, h, step], self.recv.at[way, h, step],
                    ring.right if way == 0 else ring.left,
                )
                copy.start()
                self.now[way, h] = copy
                self.sent.append(copy)

    def step(self, step):
        ring = self.ring
        before = self.now
        self.now = {}
        for h in range(2):
            for way in range(2):
                before[way, h].wait_recv()
                if step == self.last and h != way:
                    continue
                origin = ring.at(-step if way == 0 else step)
                part = self.full.at[band(origin, self.m), pl.ds(h * self.w, self.w)]
                copy = remote(
                    part, part, self.send.at[way, h, step], self.recv.at[way, h, step],
                    ring.right if way == 0 else ring.left,
                )
                copy.start()
                self.now[way, h] = copy
                self.sent.append(copy)

    def finish(self):
        for copy in self.now.values():
            copy.wait_recv()
        for copy in self.sent:
            copy.wait_send()


def ring_gather_sems(n):
    return [pltpu.SemaphoreType.DMA((2, 2, n // 2))] * 2


def lanes(width):
    return 2 if (width // 4) % 128 == 0 else 1


class RingScatter:
    def __init__(self, ring, part, slots, send, recv):
        self.ring, self.part, self.slots, self.send, self.recv = ring, part, slots, send, recv
        self.m = part.shape[0] // ring.n
        self.k = lanes(part.shape[1])
        self.w = part.shape[1] // (2 * self.k)
        self.sent = []
        self.now = {}
        self.done = {}

    def columns(self, way, j):
        return pl.ds((way * self.k + j) * self.w, self.w)

    def order(self):
        return [(way, j) for j in range(self.k) for way in range(2)]

    def advance(self, chain):
        way, j = chain
        step = self.done.get(chain, 0)
        if step == self.ring.n - 1:
            return
        self.done[chain] = step + 1
        ring = self.ring
        dest = ring.at(-1 - step if way == 0 else 1 + step)
        own = self.part.at[band(dest, self.m), self.columns(way, j)]
        src = own
        if step > 0:
            self.now[chain].wait_recv()
            src = self.slots.at[way, step - 1, j]

            def add(at, i):
                src[at, :] = (src[at, :].astype(F32) + own[at, :].astype(F32)).astype(BF16)

            tiles(self.m, add)
        copy = remote(
            src, self.slots.at[way, step, j], self.send.at[way, j, step],
            self.recv.at[way, j, step], ring.right if way == 0 else ring.left,
        )
        copy.start()
        self.now[chain] = copy
        self.sent.append(copy)

    def with_product(self, product):
        for i, chain in enumerate(self.order()):
            product.columns(chain)
            self.advance(chain)
            for earlier in self.order()[:i]:
                self.advance(earlier)

    def round(self):
        for chain in self.order():
            self.advance(chain)

    def finish(self, scale, out):
        ring = self.ring
        for j in range(self.k):
            for way in range(2):
                self.now[way, j].wait_recv()
                own = self.part.at[band(ring.col, self.m), self.columns(way, j)]
                got = self.slots.at[way, ring.n - 2, j]
                columns = self.columns(way, j)

                def add(at, i, own=own, got=got, columns=columns):
                    total = got[at, :].astype(F32) + own[at, :].astype(F32)
                    if scale is not None:
                        total = total * scale[0:1, columns]
                    out[at, columns] = total.astype(BF16)

                tiles(self.m, add)
        for copy in self.sent:
            copy.wait_send()


def ring_scatter_scratch(n, tokens, width):
    k = lanes(width)
    return [
        pltpu.VMEM((2, n - 1, k, tokens // n, width // (2 * k)), BF16),
        pltpu.SemaphoreType.DMA((2, k, n - 1)),
        pltpu.SemaphoreType.DMA((2, k, n - 1)),
    ]


class Product:
    def __init__(self, sums, left, weights, held, sem):
        self.sums, self.left, self.weights, self.held, self.sem = sums, left, weights, held, sem

    def fetch(self, chain):
        way, j = chain
        at = self.sums.columns(way, j)
        source = self.weights.at[:, at]
        return pltpu.make_async_copy(source, self.held.at[way, j], self.sem.at[way, j])

    def start(self):
        for chain in self.sums.order():
            self.fetch(chain).start()

    def columns(self, chain):
        way, j = chain
        self.fetch(chain).wait()
        w = self.sums.w
        size = math.gcd(w, 256)
        first = (way * self.sums.k + j) * w

        def body(t, carry):
            at = pl.ds(pl.multiple_of(t * size, size), size)
            block = self.held[way, j, :, at]
            value = lax.dot_general(
                self.left[...], block, (((1,), (0,)), ((), ())),
                preferred_element_type=F32,
            )
            self.sums.part[:, pl.ds(pl.multiple_of(first + t * size, size), size)] = value.astype(BF16)
            return carry

        lax.fori_loop(0, w // size, body, 0)


def product_scratch(tokens, depth, width):
    k = lanes(width)
    w = width // (2 * k)
    return [
        pltpu.VMEM((2, k, depth, w), BF16),
        pltpu.SemaphoreType.DMA((2, k)),
        pltpu.VMEM((tokens, width), BF16),
    ]


class RowScatter:
    def __init__(self, rows, part, sib, out, land, send, recv):
        self.rows, self.part, self.sib, self.out, self.land = rows, part, sib, out, land
        self.send, self.recv = send, recv
        self.m = part.shape[0] // (2 * rows.groups)

    def pairs(self):
        rows = self.rows
        g = rows.groups
        self.first = []
        for d in [*range(1, g), 0]:
            chunk = rows.of(d, 1 - rows.core)
            copy = remote(
                self.part.at[band(chunk, self.m), :], self.sib.at[d], self.send.at[0, d],
                self.recv.at[0, d], rows.sibling,
            )
            copy.start()
            self.first.append((d, copy))

    def chips(self):
        rows = self.rows
        self.second = []
        for d, copy in self.first:
            copy.wait_recv()
            if d == 0:
                continue
            own = self.part.at[band(rows.of(d, rows.core), self.m), :]

            def add(at, i, d=d, own=own):
                self.out[d - 1, at, :] = (
                    own[at, :].astype(F32) + self.sib[d, at, :].astype(F32)
                ).astype(BF16)

            tiles(self.m, add)
            far = remote(
                self.out.at[d - 1], self.land.at[d - 1], self.send.at[1, d], self.recv.at[1, d],
                {"row": rows.of(d, rows.core)},
            )
            far.start()
            self.second.append(far)

    def arrived(self):
        for copy in self.second:
            copy.wait_recv()

    def total(self, at, i):
        m = self.m
        own = pl.ds(pl.multiple_of(self.rows.me * m + i * ROWS, ROWS), ROWS)
        value = self.part[own, :].astype(F32) + self.sib[0, at, :].astype(F32)
        for d in range(1, self.rows.groups):
            value += self.land[d - 1, at, :].astype(F32)
        return value

    def finish(self):
        for _, copy in self.first:
            copy.wait_send()
        for copy in self.second:
            copy.wait_send()


def row_scratch(count, tokens, width):
    g = count // 2
    m = tokens // count
    return [
        pltpu.VMEM((g, m, width), BF16),
        pltpu.VMEM((max(g - 1, 1), m, width), BF16),
        pltpu.VMEM((max(g - 1, 1), m, width), BF16),
    ] + [pltpu.SemaphoreType.DMA((2, g))] * 4


class RowGather:
    def __init__(self, rows, full, send, recv):
        self.rows, self.full, self.send, self.recv = rows, full, send, recv
        self.m = full.shape[0] // (2 * rows.groups)

    def to_sibling(self, d):
        part = self.full.at[band(self.rows.of(-d, self.rows.core), self.m), :]
        copy = remote(part, part, self.send.at[0, d], self.recv.at[0, d], self.rows.sibling)
        copy.start()
        return copy

    def start(self):
        rows = self.rows
        part = self.full.at[band(rows.me, self.m), :]
        self.far = []
        for d in range(1, rows.groups):
            copy = remote(
                part, part, self.send.at[1, d], self.recv.at[1, d], {"row": rows.of(d, rows.core)}
            )
            copy.start()
            self.far.append(copy)
        self.near = [self.to_sibling(0)]

    def forward(self):
        for d, copy in enumerate(self.far, 1):
            copy.wait_recv()
            self.near.append(self.to_sibling(d))

    def finish(self):
        for copy in self.near:
            copy.wait_recv()
        for copy in self.near + self.far:
            copy.wait_send()


def interleave(gather_step, count, row_scatter, middle, row_gather):
    row_scatter.pairs()
    row_scatter.chips()
    half = (2 * count + 2) // 3
    for s in range(1, 1 + half):
        gather_step(s)
    row_scatter.arrived()
    middle()
    row_gather.start()
    for s in range(1 + half, count + 1):
        gather_step(s)


def tokens_kernel(n, share, full, send, recv):
    ring = Ring(n)
    m = share.shape[0]
    full[band(ring.col, m), :] = share[...]
    greet(ring, None)
    gather = RingGather(ring, full, send, recv)
    gather.start(0)
    for s in range(1, n // 2):
        gather.step(s)
    gather.finish()


def forward_kernel(
    n, count, part, share, up_scale, down_scale, hidden, grad_out, pre,
    send, recv, sib, out, land, rs_send, rs_recv, ag_send, ag_recv,
):
    ring, rows = Ring(n), Rows(count)
    m = share.shape[0]
    grad_out[band(ring.col, m), :] = (share[...].astype(F32) * down_scale[0:1, :]).astype(BF16)
    greet(ring, rows)
    scatter = RowScatter(rows, part, sib, out, land, rs_send, rs_recv)
    row_gather = RowGather(rows, hidden, ag_send, ag_recv)
    gather = RingGather(ring, grad_out, send, recv)
    gather.start(0)
    mr = scatter.m

    def middle():
        def body(at, i):
            x = scatter.total(at, i) * up_scale[0:1, :]
            pre[at, :] = x
            h = 0.5 * x * (1.0 + jnp.tanh(ROOT * (x + CUBIC * (x * x * x))))
            mine = pl.ds(pl.multiple_of(rows.me * mr + i * ROWS, ROWS), ROWS)
            hidden[mine, :] = h.astype(BF16)

        tiles(mr, body)

    interleave(gather.step, n // 2 - 1, scatter, middle, row_gather)
    row_gather.forward()
    gather.finish()
    row_gather.finish()
    scatter.finish()


def backward_kernel(
    n, count, part, hidden, pre, up_scale, down_scale, down_mant, mid, output,
    held, held_sem, out_part, slots, send, recv, sib, out, land, rs_send, rs_recv, ag_send, ag_recv,
):
    ring, rows = Ring(n), Rows(count)
    greet(ring, rows)
    scatter = RowScatter(rows, part, sib, out, land, rs_send, rs_recv)
    row_gather = RowGather(rows, mid, ag_send, ag_recv)
    sums = RingScatter(ring, out_part, slots, send, recv)
    product = Product(sums, hidden, down_mant, held, held_sem)
    mr = scatter.m

    def middle():
        def body(at, i):
            up = scatter.total(at, i)
            x = pre[at, :]
            t = jnp.tanh(ROOT * (x + CUBIC * (x * x * x)))
            slope = 0.5 * (1.0 + t) + 0.5 * x * (1.0 - t * t) * (ROOT * (1.0 + 3.0 * CUBIC * (x * x)))
            mine = pl.ds(pl.multiple_of(rows.me * mr + i * ROWS, ROWS), ROWS)
            mid[mine, :] = (slope * up * up_scale[0:1, :]).astype(BF16)

        tiles(mr, body)

    scatter.pairs()
    product.start()
    scatter.chips()
    sums.with_product(product)
    scatter.arrived()
    middle()
    row_gather.start()
    for s in range(n - 2):
        sums.round()
        if s == n // 2 - 1:
            row_gather.forward()
    sums.finish(down_scale, output)
    row_gather.finish()
    scatter.finish()


def sum_kernel(n, part, result, slots, send, recv):
    ring = Ring(n)
    greet(ring, None)
    sums = RingScatter(ring, part, slots, send, recv)
    for s in range(n - 1):
        sums.round()
    sums.finish(None, result)


def call(body, outs, scratch, number, *operands, weights=()):
    spec = pl.BlockSpec(memory_space=pltpu.VMEM)
    return pl.pallas_call(
        body,
        out_shape=outs,
        in_specs=[spec] * len(operands) + [pl.BlockSpec(memory_space=pl.ANY)] * len(weights),
        out_specs=jax.tree.map(lambda _: spec, outs),
        scratch_shapes=scratch,
        compiler_params=pltpu.CompilerParams(
            collective_id=number, has_side_effects=True, vmem_limit_bytes=52 * 1024 * 1024
        ),
    )(*operands, *weights)


def outer_kernel(step, left, right, out):
    def body(j, carry):
        at = pl.ds(pl.multiple_of(j * step, step), step)
        out[:, at] = lax.dot_general(
            left[...], right[:, at], (((0,), (0,)), ((), ())), preferred_element_type=F32
        ).astype(BF16)
        return carry

    lax.fori_loop(0, right.shape[1] // step, body, 0)


def outer(left, right):
    tokens, a = left.shape
    b = right.shape[1]
    ta, tb = math.gcd(a, 512), math.gcd(b, 1024)
    return pl.pallas_call(
        functools.partial(outer_kernel, tb),
        out_shape=jax.ShapeDtypeStruct((a, b), BF16),
        grid=(a // ta,),
        in_specs=[
            pl.BlockSpec((tokens, ta), lambda i: (0, i)),
            pl.BlockSpec((tokens, b), lambda i: (0, 0)),
        ],
        out_specs=pl.BlockSpec((ta, b), lambda i: (i, 0)),
        compiler_params=pltpu.CompilerParams(vmem_limit_bytes=40 * 1024 * 1024),
        cost_estimate=pl.CostEstimate(
            flops=2 * a * b * tokens, bytes_accessed=2 * (a * b + tokens * (a + b)), transcendentals=0
        ),
    )(left, right)


def shards(n, count, tokens, up_mant, up_exp, down_mant, down_exp, cotangent):
    struct = jax.ShapeDtypeStruct
    m, width = tokens.shape
    units = up_mant.shape[1]
    total = m * n
    up_scale = jnp.exp2(up_exp.astype(F32))[None, :]
    down_scale = jnp.exp2(down_exp.astype(F32))[None, :]
    x_full = call(
        functools.partial(tokens_kernel, n), struct((total, width), BF16), ring_gather_sems(n), 0, tokens
    )
    up_term = jnp.dot(x_full, up_mant, preferred_element_type=F32).astype(BF16)
    hidden, grad_out, pre = call(
        functools.partial(forward_kernel, n, count),
        (struct((total, units), BF16), struct((total, width), BF16), struct((total // count, units), F32)),
        ring_gather_sems(n) + row_scratch(count, total, units),
        1, up_term, cotangent, up_scale, down_scale,
    )
    back_term = lax.dot_general(
        grad_out, down_mant, (((1,), (1,)), ((), ())), preferred_element_type=F32
    ).astype(BF16)
    mid, output = call(
        functools.partial(backward_kernel, n, count),
        (struct((total, units), BF16), struct((m, width), BF16)),
        product_scratch(total, units, width)
        + ring_scatter_scratch(n, total, width)
        + row_scratch(count, total, units),
        2, back_term, hidden, pre, up_scale, down_scale, weights=(down_mant,),
    )
    tokens_term = lax.dot_general(
        mid, up_mant, (((1,), (1,)), ((), ())), preferred_element_type=F32
    ).astype(BF16)
    grad_tokens = call(
        functools.partial(sum_kernel, n), struct((m, width), BF16),
        ring_scatter_scratch(n, total, width), 3, tokens_term,
    )
    return (output, grad_tokens, outer(x_full, mid), outer(hidden, grad_out))


def solution(mesh):
    placed = (P("col", "row"), P("row", "col"), P("col"), P("col", "row"), P("row"), P("col", "row"))
    return jax.shard_map(
        functools.partial(shards, mesh.shape["col"], mesh.shape["row"]),
        mesh=mesh,
        in_specs=placed,
        out_specs=(P("col", "row"), P("col", "row"), P("row", "col"), P("col", "row")),
        check_vma=False,
    )
```
